256 devices in a mesh: seq: 16 (over y, z_hi), tp: 16 (over z_lo, x, core).
Axes of the slice: x: 4, y: 4, z: 8 (z_hi: 4, z_lo: 2; z = z_hi * 2 + z_lo), core: 2. Of those that a mesh axis runs over, the one named last changes fastest.
Arguments:
- spatial_input_rows: bfloat16 [2, 16, 128, 3072], P(None, 'seq', None, 'tp'), may hold values from -6 to 6
- x_temporal: bfloat16 [2, 16, 128, 3072], P(None, 'seq', None, 'tp'), may hold values from -6 to 6
- cotangent: bfloat16 [2, 16, 128, 3072], P(None, 'seq', None, 'tp'), may hold values from -6 to 6
- spatial_query_key_value: bfloat16 [3072, 3, 2048], P(None, None, 'tp'), may hold values from -0.109375 to 0.109375
- spatial_output_weight: bfloat16 [2048, 3072], P('tp'), may hold values from -0.125 to 0.125
- temporal_query_key_value: bfloat16 [3072, 3, 2048], P(None, None, 'tp'), may hold values from -0.109375 to 0.109375
- temporal_output_weight: bfloat16 [2048, 3072], P('tp'), may hold values from -0.125 to 0.125
- up_weight: bfloat16 [3072, 6144], P(None, 'tp'), may hold values from -0.109375 to 0.109375
- down_weight: bfloat16 [6144, 3072], P('tp'), may hold values from -0.078125 to 0.078125
Outputs:
- spatial_input_gradient: bfloat16 [2, 16, 128, 3072], P(None, 'seq', None, 'tp')
- grad_qkv_spatial: bfloat16 [3072, 3, 2048], P('seq', None, 'tp')
- grad_out_spatial: bfloat16 [2048, 3072], P('tp', 'seq')
- grad_qkv_temporal: bfloat16 [3072, 3, 2048], P('seq', None, 'tp')
- grad_out_temporal: bfloat16 [2048, 3072], P('tp', 'seq')
- grad_up: bfloat16 [3072, 6144], P('seq', 'tp')
- grad_down: bfloat16 [6144, 3072], P('tp', 'seq')
The draws below stay inside these ranges and needn't reach their ends.
All inputs are finite; a program needn't handle non-finite values.
Results may differ from the reference program's by a relative error of at most 0.04.
Values may be sent and summed in bfloat16 or wider, within the bound.
No kernel may reach another device: no remote copies, remote signals or barrier semaphores. Data moves between devices by JAX's collectives and lax.ppermute only.
A program may use at most 128 MiB of HBM per device.

```python
import math
import jax
import jax.numpy as jnp
from jax import lax

D = 3072
HDIM = 128
HEADS = 16
FF = 6144
FRAMES = 16
PATCHES = 128
SEQS = 2
N_SEQ = 16
N_TP = 16


def strengthened(array, rng, source, target, parts, factor):
    owner, partner = [(jnp.arange(array.shape[position]) // (array.shape[position] // parts)).reshape([-1 if axis == position else 1 for axis in range(array.ndim)]) for position in (source, target)]
    chosen = jax.random.permutation(rng, parts)[partner]
    strong = (owner == chosen) | (owner == (partner + parts // 2) % parts)
    return jnp.where(strong, factor * array, array)


def steps_of(own_key, dims, pieces, least, top_value):
    factor_of, own = 1.0, jax.random.fold_in(own_key, 6)
    for axis_at, blocks in pieces:
        draws = jnp.exp(jax.random.uniform(jax.random.fold_in(own, axis_at), (blocks,), jnp.float32, least / len(pieces), top_value / len(pieces)))
        factor_of = factor_of * jnp.repeat(draws, dims[axis_at] // blocks).reshape([-1 if axis == axis_at else 1 for axis in range(len(dims))])
    return factor_of


def scatter_about(key, shape, scale, limit, shards=(), kind=jnp.bfloat16):
    array = scale * jax.random.normal(key, shape, jnp.float32)
    if shards:
        array = array * steps_of(key, shape, shards, -0.22, 0.18)
    return jnp.clip(array, -limit, limit).astype(kind)


def gaussian_with(stream_key, dims, deviation, limit, pieces, heavy, kind=jnp.bfloat16):
    array = deviation * jax.random.normal(stream_key, dims, jnp.float32)
    if pieces:
        array = array * steps_of(stream_key, dims, pieces, -0.22, 0.18)
    return jnp.clip(strengthened(array, jax.random.fold_in(stream_key, 3), *heavy), -limit, limit).astype(kind)


def setup_inputs(seed: int = 0) -> dict:
    key_list = jax.random.split(jax.random.key(seed), 10)
    return {
        "spatial_input_rows": scatter_about(key_list[0], (SEQS, FRAMES, PATCHES, D), 1.0, 6.0, ((1, 16), (3, 16))),
        "x_temporal": scatter_about(key_list[1], (SEQS, FRAMES, PATCHES, D), 1.0, 6.0, ((1, 16), (3, 16))),
        "cotangent": gaussian_with(key_list[2], (SEQS, FRAMES, PATCHES, D), 1.0, 6.0, ((1, 16), (3, 16)), (1, 3, 16, 2.0)),
        "spatial_query_key_value": scatter_about(key_list[3], (D, 3, HEADS * HDIM), D ** -0.5, 0.109375, ((2, 16),)),
        "spatial_output_weight": scatter_about(key_list[4], (HEADS * HDIM, D), (HEADS * HDIM) ** -0.5, 0.125, ((0, 16),)),
        "temporal_query_key_value": scatter_about(key_list[5], (D, 3, HEADS * HDIM), D ** -0.5, 0.109375, ((2, 16),)),
        "temporal_output_weight": scatter_about(key_list[6], (HEADS * HDIM, D), (HEADS * HDIM) ** -0.5, 0.125, ((0, 16),)),
        "up_weight": scatter_about(key_list[7], (D, FF), D ** -0.5, 0.109375, ((1, 16),)),
        "down_weight": scatter_about(key_list[8], (FF, D), FF ** -0.5, 0.078125, ((0, 16),)),
    }


EPS = 1e-06
ROOT = 0.7978845608028654
CUBIC = 0.044715

def gelu_value(pre_act):
    inner_product = jnp.tanh(ROOT * (pre_act + CUBIC * pre_act * pre_act * pre_act))
    return 0.5 * pre_act * (1.0 + inner_product)

def gelu_slope(pre_act):
    inner_product = jnp.tanh(ROOT * (pre_act + CUBIC * pre_act * pre_act * pre_act))
    return 0.5 * (1.0 + inner_product) + 0.5 * pre_act * (1.0 - inner_product * inner_product) * ROOT * (1.0 + 3.0 * CUBIC * pre_act * pre_act)

def apply_norm(values):
    wide = values.astype(jnp.float32)
    inverse_norm = lax.rsqrt(lax.optimization_barrier(jnp.mean(wide * wide, axis=-1, keepdims=True)) + EPS)
    return (inverse_norm, wide * inverse_norm)

def norm_reverse_pass(residual_stream, inverse_norm, centered_rows, gradient_norm_rows):
    inner_product = lax.optimization_barrier(jnp.mean(gradient_norm_rows * centered_rows, axis=-1, keepdims=True))
    return (residual_stream.astype(jnp.float32) + inverse_norm * (gradient_norm_rows - centered_rows * inner_product)).astype(jnp.bfloat16)

def group_sum(left, right):
    width = left.shape[2] // N_TP
    lead = left.shape[1]

    def step(running_total, index):
        start = index * width
        piece = lax.dynamic_slice_in_dim(left, start, width, 2).reshape(left.shape[0], lead * width)
        block = lax.dynamic_slice_in_dim(right, start, width, 1).reshape(lead * width, right.shape[2])
        term = jnp.dot(piece, block, preferred_element_type=jnp.float32).astype(jnp.bfloat16)
        term = lax.optimization_barrier(term)
        return (running_total + term.astype(jnp.float32), None)
    start_total = jnp.zeros((left.shape[0], right.shape[2]), jnp.float32)
    running_total, discarded_value = lax.scan(step, start_total, jnp.arange(N_TP, dtype=jnp.int32))
    return running_total

def shard_sum(left, right, scale_factor):
    span = left.shape[1] // N_SEQ

    def step(running_total, index):
        piece = lax.dynamic_slice_in_dim(left, index * span, span, 1).reshape(-1, left.shape[3])
        other = lax.dynamic_slice_in_dim(right, index * span, span, 1).reshape(-1, right.shape[3])
        term = (scale_factor * jnp.dot(piece.T, other, preferred_element_type=jnp.float32)).astype(jnp.bfloat16)
        term = lax.optimization_barrier(term)
        return (running_total + term.astype(jnp.float32), None)
    start_total = jnp.zeros((left.shape[3], right.shape[3]), jnp.float32)
    running_total, discarded_value = lax.scan(step, start_total, jnp.arange(N_SEQ, dtype=jnp.int32))
    return running_total.astype(jnp.bfloat16)

def attention_forward(normed_rows, weights):
    lead = normed_rows.shape[:3]
    joined = jnp.einsum('bgld,dkh->bglkh', normed_rows.astype(jnp.float32), weights.astype(jnp.float32)).astype(jnp.bfloat16)
    joined = joined.reshape(lead + (3, HEADS, HDIM))
    query = joined[:, :, :, 0]
    keyset = joined[:, :, :, 1]
    values = joined[:, :, :, 2]
    scores = jnp.einsum('bgqnh,bgknh->bgnqk', query.astype(jnp.float32), keyset.astype(jnp.float32)) / math.sqrt(HDIM)
    row_max = lax.optimization_barrier(jnp.max(scores, axis=-1, keepdims=True))
    raised = jnp.exp(scores - row_max)
    attn_prob = raised / lax.optimization_barrier(jnp.sum(raised, axis=-1, keepdims=True))
    attn_weights = attn_prob.astype(jnp.bfloat16)
    context = jnp.einsum('bgnqk,bgknh->bgqnh', attn_weights.astype(jnp.float32), values.astype(jnp.float32)).astype(jnp.bfloat16)
    return (query, keyset, values, attn_prob, attn_weights, context.reshape(lead + (HEADS * HDIM,)))

def layer_reverse_pass(normed_rows, inverse_norm, centered_rows, portion_count, incoming_gradient, query_key_value_weight, output_matrix, scale_factor):
    query, keyset, values, attn_prob, attn_weights, context = portion_count
    lead = incoming_gradient.shape[:3]
    count = lead[0] * lead[1] * lead[2]
    d_context = jnp.dot(incoming_gradient.reshape(count, D), output_matrix.T, preferred_element_type=jnp.float32).astype(jnp.bfloat16)
    d_heads = d_context.reshape(query.shape)
    d_values = jnp.einsum('bgnqk,bgqnh->bgknh', attn_weights.astype(jnp.float32), d_heads.astype(jnp.float32)).astype(jnp.bfloat16)
    d_probs = jnp.einsum('bgqnh,bgknh->bgnqk', d_heads.astype(jnp.float32), values.astype(jnp.float32))
    d_scores = (attn_prob * (d_probs - lax.optimization_barrier(jnp.sum(attn_prob * d_probs, axis=-1, keepdims=True))) / math.sqrt(HDIM)).astype(jnp.bfloat16)
    d_query = jnp.einsum('bgnqk,bgknh->bgqnh', d_scores.astype(jnp.float32), keyset.astype(jnp.float32)).astype(jnp.bfloat16)
    d_keys = jnp.einsum('bgnqk,bgqnh->bgknh', d_scores.astype(jnp.float32), query.astype(jnp.float32)).astype(jnp.bfloat16)
    d_qkv = jnp.stack((d_query, d_keys, d_values), axis=3).reshape(lead + (3 * HEADS * HDIM,))
    projection_gradient = shard_sum(normed_rows, d_qkv, scale_factor).reshape(D, 3, HEADS * HDIM)
    output_weight_gradient = shard_sum(context, incoming_gradient, scale_factor)
    norm_gradient = group_sum(d_qkv.reshape(count, 3, HEADS * HDIM), jnp.transpose(query_key_value_weight, (1, 2, 0)))
    return (norm_reverse_pass(incoming_gradient, inverse_norm, centered_rows, norm_gradient.reshape(incoming_gradient.shape)), projection_gradient, output_weight_gradient)

def reference(spatial_input_rows, x_temporal, cotangent, spatial_query_key_value, spatial_output_weight, temporal_query_key_value, temporal_output_weight, up_weight, down_weight):
    count = SEQS * FRAMES * PATCHES
    scale_factor = count ** (-0.5)
    temporal_state = jnp.transpose(x_temporal, (0, 2, 1, 3))
    upstream_gradient = jnp.transpose(cotangent, (0, 2, 1, 3))
    lead = temporal_state.shape[:3]
    temporal_inverse_norm, temporal_centered_rows = apply_norm(temporal_state)
    temporal_normed_rows = temporal_centered_rows.astype(jnp.bfloat16)
    temporal_portions = attention_forward(temporal_normed_rows, temporal_query_key_value)
    attn_out = group_sum(temporal_portions[5].reshape(count, 1, HEADS * HDIM), temporal_output_weight[None])
    middle_state = (temporal_state.astype(jnp.float32) + attn_out.reshape(temporal_state.shape)).astype(jnp.bfloat16)
    mlp_inverse_norm, mlp_centered_rows = apply_norm(middle_state)
    mlp_normed_rows = mlp_centered_rows.astype(jnp.bfloat16)
    pre_act = jnp.dot(mlp_normed_rows.reshape(count, D), up_weight, preferred_element_type=jnp.float32)
    hidden = gelu_value(pre_act).astype(jnp.bfloat16)
    d_act = jnp.dot(upstream_gradient.reshape(count, D), down_weight.T, preferred_element_type=jnp.float32)
    d_pre = (d_act * gelu_slope(pre_act)).astype(jnp.bfloat16)
    grad_down = shard_sum(hidden.reshape(lead + (FF,)), upstream_gradient, scale_factor)
    grad_up = shard_sum(mlp_normed_rows, d_pre.reshape(lead + (FF,)), scale_factor)
    mlp_norm_gradient = group_sum(d_pre.reshape(count, 1, FF), up_weight.T[None])
    middle_gradient = norm_reverse_pass(upstream_gradient, mlp_inverse_norm, mlp_centered_rows, mlp_norm_gradient.reshape(temporal_state.shape))
    temporal_gradient, temporal_projection_gradient, temporal_output_gradient = layer_reverse_pass(temporal_normed_rows, temporal_inverse_norm, temporal_centered_rows, temporal_portions, middle_gradient, temporal_query_key_value, temporal_output_weight, scale_factor)
    frame_gradient = jnp.transpose(temporal_gradient, (0, 2, 1, 3))
    spatial_inverse_norm, spatial_centered_rows = apply_norm(spatial_input_rows)
    spatial_normed_rows = spatial_centered_rows.astype(jnp.bfloat16)
    spatial_portions = attention_forward(spatial_normed_rows, spatial_query_key_value)
    spatial_input_gradient, spatial_projection_gradient, spatial_output_gradient = layer_reverse_pass(spatial_normed_rows, spatial_inverse_norm, spatial_centered_rows, spatial_portions, frame_gradient, spatial_query_key_value, spatial_output_weight, scale_factor)
    return (spatial_input_gradient, spatial_projection_gradient, spatial_output_gradient, temporal_projection_gradient, temporal_output_gradient, grad_up, grad_down)
```

```python
import math

import jax
import jax.numpy as jnp
from jax import lax
from jax.sharding import Mesh
from jax.sharding import PartitionSpec as P

D = 3072
HDIM = 128
FRAMES = 16
PATCHES = 128
SEQS = 2
TOKENS = 256
HALF = 128
CHIPS = 8
EPS = 1e-06
ROOT = 0.7978845608028654
CUBIC = 0.044715
SCALE = (SEQS * FRAMES * PATCHES) ** -0.5
SEQ = ("y", "zh")
TP = ("zl", "x", "c")
RING = ("zl", "x")


def gelu_both(pre_act):
    inner = jnp.tanh(ROOT * (pre_act + CUBIC * pre_act * pre_act * pre_act))
    value = 0.5 * pre_act * (1.0 + inner)
    slope = 0.5 * (1.0 + inner) + 0.5 * pre_act * (1.0 - inner * inner) * ROOT * (
        1.0 + 3.0 * CUBIC * pre_act * pre_act
    )
    return value, slope


def dot(left, right, dims):
    return lax.dot_general(left, right, (dims, ((), ())), preferred_element_type=jnp.float32)


def mm(left, right):
    return dot(left, right, ((1,), (0,)))


def mm_nt(left, right):
    return dot(left, right, ((1,), (1,)))


def mm_tn(left, right):
    return dot(left, right, ((0,), (0,)))


def half(values):
    return values.astype(jnp.bfloat16)


def wide(values):
    return values.astype(jnp.float32)


def normalize(values):
    values = wide(values)
    inverse = lax.rsqrt(jnp.mean(values * values, axis=-1, keepdims=True) + EPS)
    return inverse, values * inverse


def normalize_back(residual, inverse, centered, gradient):
    inner = jnp.mean(gradient * centered, axis=-1, keepdims=True)
    return half(wide(residual) + inverse * (gradient - centered * inner))


def swap(values):
    return lax.ppermute(values, "c", [(0, 1), (1, 0)])


def spread(values):
    copies = jnp.broadcast_to(values[None], (CHIPS,) + values.shape)
    return lax.all_to_all(copies, RING, 0, 0, tiled=True)


def features_whole(values):
    count = values.shape[1]
    theirs = swap(values[1])
    first = lax.axis_index("c") == 0
    low = jnp.where(first, values[0], theirs)
    high = jnp.where(first, theirs, values[0])
    joined = jnp.concatenate((low, high), axis=1)
    return jnp.transpose(spread(joined), (1, 0, 2)).reshape(count, D)


def own_first(values):
    core = lax.axis_index("c")
    return jnp.where(core == 0, values, values[::-1])


def both(values):
    return jnp.concatenate((values, swap(values)), axis=0)


def rows_whole(values):
    return both(spread(values).reshape(HALF, D))


def reduce_rows(left, right):
    theirs = swap(half(mm_nt(left[HALF:], right)))
    mine = half(mm_nt(left[:HALF], right) + wide(theirs))
    pieces = lax.all_to_all(mine.reshape(CHIPS, HALF // CHIPS, D), RING, 0, 0, tiled=True)
    return jnp.sum(wide(pieces), axis=0)


def sum_tokens(term):
    pieces = lax.all_to_all(term.reshape(4, D // 4, -1), "y", 0, 0, tiled=True)
    part = half(jnp.sum(wide(pieces), axis=0))
    pieces = lax.all_to_all(part.reshape(4, D // 16, -1), "zh", 0, 0, tiled=True)
    return half(jnp.sum(wide(pieces), axis=0))


def own_rows(values):
    chip = lax.axis_index(RING)
    count = HALF // CHIPS
    return lax.dynamic_slice_in_dim(values[:HALF], chip * count, count, 0)


def attend(normed, weight, span):
    joined = half(mm(normed, weight))
    query, keyset, values = joined[:, :HDIM], joined[:, HDIM : 2 * HDIM], joined[:, 2 * HDIM :]
    scores = mm_nt(query, keyset) / math.sqrt(HDIM)
    group = jnp.arange(TOKENS) // span
    inside = group[:, None] == group[None, :]
    scores = jnp.where(inside, scores, -jnp.inf)
    raised = jnp.exp(scores - jnp.max(scores, axis=-1, keepdims=True))
    prob = raised / jnp.sum(raised, axis=-1, keepdims=True)
    weights = half(prob)
    context = half(mm(weights, values))
    return query, keyset, values, prob, weights, context


def attend_back(saved, gradient, output_weight):
    query, keyset, values, prob, weights, context = saved
    d_context = half(mm_nt(gradient, output_weight))
    d_values = half(mm_tn(weights, d_context))
    d_probs = mm_nt(d_context, values)
    d_scores = half(
        prob * (d_probs - jnp.sum(prob * d_probs, axis=-1, keepdims=True)) / math.sqrt(HDIM)
    )
    d_query = half(mm(d_scores, keyset))
    d_keys = half(mm_tn(d_scores, query))
    return jnp.concatenate((d_query, d_keys, d_values), axis=1)


def weight_terms(left, right):
    return half(SCALE * mm_tn(left, right))


def per_device(
    spatial_input_rows,
    x_temporal,
    cotangent,
    spatial_query_key_value,
    spatial_output_weight,
    temporal_query_key_value,
    temporal_output_weight,
    up_weight,
    down_weight,
):
    width = D // 16
    qkv_t = temporal_query_key_value.reshape(D, 3 * HDIM)
    qkv_s = spatial_query_key_value.reshape(D, 3 * HDIM)

    pair = jnp.stack((x_temporal[:, 0], cotangent[:, 0])).reshape(2, 2, 16, 8, width)
    pair = lax.all_to_all(jnp.transpose(pair, (2, 0, 1, 3, 4)), SEQ, 0, 0, tiled=True)
    pair = jnp.transpose(pair, (2, 1, 3, 0, 4)).reshape(2, 2 * HALF, width)
    pair = features_whole(own_first(pair))
    both_pair = jnp.stack((pair, swap(pair))).reshape(2, 2, HALF, D)
    x_rows = both_pair[:, 0].reshape(TOKENS, D)
    upstream = both_pair[:, 1].reshape(TOKENS, D)

    inverse_t, centered_t = normalize(x_rows)
    normed_t = half(centered_t)
    saved_t = attend(normed_t, qkv_t, FRAMES)
    context_t = saved_t[5]
    attn_own = reduce_rows(context_t, temporal_output_weight.T)
    x_own = own_rows(x_rows)
    inverse_own, centered_own = normalize(x_own)

    middle_own = half(wide(x_own) + attn_own)
    inverse_m, centered_m = normalize(middle_own)
    normed_m = rows_whole(half(centered_m))
    value, slope = gelu_both(mm(normed_m, up_weight))
    hidden = half(value)
    d_pre = half(mm_nt(upstream, down_weight) * slope)
    d_norm_m = reduce_rows(d_pre, up_weight)
    mlp_terms = jnp.concatenate(
        (weight_terms(normed_m, d_pre), weight_terms(upstream, hidden)), axis=1
    )
    mlp_grads = sum_tokens(mlp_terms)
    d_middle_own = normalize_back(own_rows(upstream), inverse_m, centered_m, d_norm_m)
    d_middle = rows_whole(d_middle_own)

    d_qkv_t = attend_back(saved_t, d_middle, temporal_output_weight)
    d_norm_t = reduce_rows(d_qkv_t, qkv_t)
    temporal_terms = jnp.concatenate(
        (weight_terms(normed_t, d_qkv_t), weight_terms(d_middle, context_t)), axis=1
    )
    temporal_grads = sum_tokens(temporal_terms)
    d_temporal_own = normalize_back(d_middle_own, inverse_own, centered_own, d_norm_t)

    d_frame_own = lax.all_to_all(d_temporal_own, SEQ, 0, 0, tiled=True)
    d_frame = rows_whole(d_frame_own)

    rows = jnp.transpose(spatial_input_rows.reshape(2, 16, 8, width), (0, 2, 1, 3))
    s_rows = both(features_whole(own_first(rows.reshape(2, HALF, width))))
    inverse_s, centered_s = normalize(s_rows)
    normed_s = half(centered_s)
    saved_s = attend(normed_s, qkv_s, PATCHES)
    d_qkv_s = attend_back(saved_s, d_frame, spatial_output_weight)
    spatial_terms = jnp.concatenate(
        (weight_terms(normed_s, d_qkv_s), weight_terms(d_frame, saved_s[5])), axis=1
    )
    spatial_grads = sum_tokens(spatial_terms)
    d_norm_s = reduce_rows(d_qkv_s, qkv_s)
    inverse_own_s, centered_own_s = normalize(own_rows(s_rows))
    result_own = normalize_back(d_frame_own, inverse_own_s, centered_own_s, d_norm_s)
    result = jnp.transpose(result_own.reshape(16, 16, width), (1, 0, 2))
    result = lax.all_to_all(result, TP, 0, 0, tiled=True)
    result = jnp.transpose(result.reshape(8, 2, 16, width), (1, 2, 0, 3))

    split = 3 * HDIM
    return (
        result.reshape(2, 1, PATCHES, width),
        spatial_grads[:, :split].reshape(-1, 3, HDIM),
        spatial_grads[:, split:].T,
        temporal_grads[:, :split].reshape(-1, 3, HDIM),
        temporal_grads[:, split:].T,
        mlp_grads[:, :split],
        mlp_grads[:, split:].T,
    )


def solution(mesh):
    fine = Mesh(mesh.devices.reshape(4, 4, 2, 4, 2), SEQ + TP)
    stream = P(None, SEQ, None, TP)
    return jax.shard_map(
        per_device,
        mesh=fine,
        in_specs=(
            stream,
            stream,
            stream,
            P(None, None, TP),
            P(TP, None),
            P(None, None, TP),
            P(TP, None),
            P(None, TP),
            P(TP, None),
        ),
        out_specs=(
            stream,
            P(SEQ, None, TP),
            P(TP, SEQ),
            P(SEQ, None, TP),
            P(TP, SEQ),
            P(SEQ, TP),
            P(TP, SEQ),
        ),
        check_vma=False,
    )
```

```python
import math

import jax
import jax.numpy as jnp
from jax import lax
from jax.sharding import Mesh
from jax.sharding import PartitionSpec as P

D = 3072
HDIM = 128
FRAMES = 16
PATCHES = 128
SEQS = 2
TOKENS = 256
HALF = 128
CHIPS = 8
EPS = 1e-06
ROOT = 0.7978845608028654
CUBIC = 0.044715
SCALE = (SEQS * FRAMES * PATCHES) ** -0.5
SEQ = ("y", "zh")
TP = ("zl", "x", "c")
RING = ("zl", "x")
PAIRS = ((0, 1), (1, 0), (2, 3), (3, 2))
CROSS = ((1, 2), (2, 1), (3, 0), (0, 3))


def gelu_both(pre_act):
    inner = jnp.tanh(ROOT * (pre_act + CUBIC * pre_act * pre_act * pre_act))
    value = 0.5 * pre_act * (1.0 + inner)
    slope = 0.5 * (1.0 + inner) + 0.5 * pre_act * (1.0 - inner * inner) * ROOT * (
        1.0 + 3.0 * CUBIC * pre_act * pre_act
    )
    return value, slope


def dot(left, right, dims):
    return lax.dot_general(left, right, (dims, ((), ())), preferred_element_type=jnp.float32)


def mm(left, right):
    return dot(left, right, ((1,), (0,)))


def mm_nt(left, right):
    return dot(left, right, ((1,), (1,)))


def mm_tn(left, right):
    return dot(left, right, ((0,), (0,)))


def half(values):
    return values.astype(jnp.bfloat16)


def wide(values):
    return values.astype(jnp.float32)


def normalize(values):
    values = wide(values)
    inverse = lax.rsqrt(jnp.mean(values * values, axis=-1, keepdims=True) + EPS)
    return inverse, values * inverse


def normalize_back(residual, inverse, centered, gradient):
    inner = jnp.mean(gradient * centered, axis=-1, keepdims=True)
    return half(wide(residual) + inverse * (gradient - centered * inner))


def swap(values):
    return lax.ppermute(values, "c", [(0, 1), (1, 0)])


def spread(values):
    copies = jnp.broadcast_to(values[None], (CHIPS,) + values.shape)
    return lax.all_to_all(copies, RING, 0, 0, tiled=True)


def join_cores(values):
    theirs = swap(values[1])
    first = lax.axis_index("c") == 0
    low = jnp.where(first, values[0], theirs)
    high = jnp.where(first, theirs, values[0])
    return jnp.concatenate((low, high), axis=1)


def gather_z(values):
    theirs = lax.ppermute(values, "zl", [(0, 1), (1, 0)])
    first = lax.axis_index("zl") == 0
    return jnp.stack((jnp.where(first, values, theirs), jnp.where(first, theirs, values)))[:, None]


def gather_x(values, perm, first):
    theirs = lax.ppermute(values, "x", perm)
    low, high = jnp.where(first, values, theirs), jnp.where(first, theirs, values)
    return jnp.concatenate((low, high), axis=1)


def gather_pairs(values):
    return gather_x(values, PAIRS, lax.axis_index("x") % 2 == 0)


def gather_cross(values):
    values = gather_x(values, CROSS, lax.axis_index("x") < 2)
    return values.reshape((CHIPS,) + values.shape[2:])


def own_first(values):
    core = lax.axis_index("c")
    return jnp.where(core == 0, values, values[::-1])


def both(values):
    values = values.reshape(HALF, D)
    return values, swap(values)


def rows_term(left, right):
    theirs = swap(half(mm_nt(left[HALF:], right)))
    mine = half(mm_nt(left[:HALF], right) + wide(theirs))
    return mine.reshape(CHIPS, HALF // CHIPS, D)


def exchange(pieces):
    return lax.all_to_all(pieces, RING, 0, 0, tiled=True)


def rows_sum(pieces):
    return jnp.sum(wide(pieces), axis=0)


def part(order, blocks):
    count = order.shape[0] // 2
    chosen = [lax.dynamic_index_in_dim(blocks, order[i], 0) for i in range(2 * count)]
    return jnp.concatenate(chosen[:count]), jnp.concatenate(chosen[count:])


def products(order, pairs):
    terms = []
    for left, right, width, spot in pairs:
        left = jnp.concatenate(left, axis=0)
        right = right[:, spot * width : (spot + 1) * width]
        terms.append(half(SCALE * mm_tn(left, right)))
    total = jnp.concatenate(terms, axis=1)
    return part(order, total.reshape(4, D // 4, -1))


def add_and_part(order, kept, came):
    total = half(wide(kept) + wide(came))
    if total.shape[0] == 1:
        total = total.reshape(4, total.shape[1] // 4, total.shape[2])
    return part(order, total)


def beside(chunks):
    return jnp.concatenate([chunks[i] for i in range(CHIPS)], axis=1)


def rows_of_chunks(own, other, norm):
    rows = jnp.concatenate((beside(own), beside(other)), axis=0)
    return half(normalize(rows)[1]) if norm else rows


class Sum:
    def __init__(self, ends):
        self.perms = (PAIRS, CROSS) if ends else (CROSS, PAIRS)
        self.orders = {}
        for axis in ("y", "zh"):
            spot = lax.axis_index(axis)
            even = spot % 2 == 0
            if ends:
                outer = (spot == 0) | (spot == 3)
                four = jnp.where(outer, jnp.array((1, 2, 3, 0)), jnp.array((3, 0, 1, 2)))
                two = jnp.where(even, jnp.array((0, 1)), jnp.array((1, 0)))
            else:
                four = jnp.where(spot < 2, jnp.array((2, 3, 0, 1)), jnp.array((0, 1, 2, 3)))
                two = jnp.where(even, jnp.array((1, 0)), jnp.array((0, 1)))
            self.orders[axis] = four.astype(jnp.int32), two.astype(jnp.int32)

    def start(self, pairs):
        self.step = 0
        sent, self.kept = products(self.orders["y"][0], pairs)
        return self.go(sent)

    def go(self, sent):
        axis = "y" if self.step < 2 else "zh"
        self.came = lax.ppermute(sent, axis, self.perms[self.step % 2])
        self.step += 1
        return sent

    def next(self, gate):
        came = after(self.came, gate)
        axis = "y" if self.step < 2 else "zh"
        if self.step == 4:
            return half(wide(self.kept[0]) + wide(came[0]))
        order = self.orders[axis][0 if self.step == 2 else 1]
        sent, self.kept = add_and_part(order, self.kept, came)
        return self.go(sent)


def next_of(sums, gate):
    return [total.next(gate) for total in sums]


def after(values, gate):
    return lax.optimization_barrier((values, gate))[0]


def along(values, *work):
    return lax.optimization_barrier((values,) + work)[0]


def row_grads(first, second):
    projection = jnp.concatenate((first, second[:, :HDIM]), axis=1)
    return projection.reshape(-1, 3, HDIM), second[:, HDIM:].T


def own_rows(values):
    chip = lax.axis_index(RING)
    count = HALF // CHIPS
    if values.ndim == 3:
        return beside(lax.dynamic_slice_in_dim(values, chip * count, count, 1))
    return lax.dynamic_slice_in_dim(values[:HALF], chip * count, count, 0)


def attend(normed, weight, span):
    joined = half(mm(normed, weight))
    query, keyset, values = joined[:, :HDIM], joined[:, HDIM : 2 * HDIM], joined[:, 2 * HDIM :]
    scores = mm_nt(query, keyset) / math.sqrt(HDIM)
    group = jnp.arange(TOKENS) // span
    scores = jnp.where(group[:, None] == group[None, :], scores, -jnp.inf)
    raised = jnp.exp(scores - jnp.max(scores, axis=-1, keepdims=True))
    prob = raised / jnp.sum(raised, axis=-1, keepdims=True)
    return joined, prob, half(mm(half(prob), values))


def attend_back(saved, own, other, output_weight):
    joined, prob, _ = saved
    gradient = jnp.concatenate((own, other), axis=0)
    d_context = half(mm_nt(gradient, output_weight))
    query, keyset, values = joined[:, :HDIM], joined[:, HDIM : 2 * HDIM], joined[:, 2 * HDIM :]
    d_values = half(mm_tn(half(prob), d_context))
    d_probs = mm_nt(d_context, values)
    inner = jnp.sum(prob * d_probs, axis=-1, keepdims=True)
    d_scores = half(prob * (d_probs - inner) / math.sqrt(HDIM))
    d_query = half(mm(d_scores, keyset))
    d_keys = half(mm_tn(d_scores, query))
    return jnp.concatenate((d_query, d_keys, d_values), axis=1)


def mlp(own, other, weight, d_act):
    normed = jnp.concatenate((own, other), axis=0)
    value, slope = gelu_both(mm(normed, weight))
    return half(d_act * slope), half(value)


def row_pairs(normed, d_joined, gradient, context):
    first = ((normed, d_joined, 2 * HDIM, 0),)
    return first, ((normed, d_joined, HDIM, 2), (gradient, context, HDIM, 0))


def per_device(
    spatial_input_rows,
    x_temporal,
    cotangent,
    spatial_query_key_value,
    spatial_output_weight,
    temporal_query_key_value,
    temporal_output_weight,
    up_weight,
    down_weight,
):
    width = D // 16
    qkv_t = temporal_query_key_value.reshape(D, 3 * HDIM)
    qkv_s = spatial_query_key_value.reshape(D, 3 * HDIM)

    pair = jnp.stack((x_temporal[:, 0], cotangent[:, 0])).reshape(2, 2, 16, 8, width)
    pair = jnp.transpose(pair, (2, 0, 1, 3, 4))
    s_part = jnp.transpose(spatial_input_rows.reshape(2, 16, 8, width), (0, 2, 1, 3))
    s_part = join_cores(own_first(s_part.reshape(2, HALF, width)))
    pair, s_part = lax.optimization_barrier((pair, s_part))
    pair = lax.all_to_all(pair, SEQ, 0, 0, tiled=True)
    s_part = gather_pairs(gather_z(s_part))
    pair, qkv_t, qkv_s, s_part = lax.optimization_barrier((pair, qkv_t, qkv_s, s_part))
    pair = jnp.transpose(pair, (2, 1, 3, 0, 4)).reshape(2, 2 * HALF, width)
    pair = join_cores(own_first(pair))
    x_chunks, u_part = lax.optimization_barrier((spread(pair[:HALF]), pair[HALF:]))

    u_chunks = spread(u_part)
    normed_t = rows_of_chunks(x_chunks, swap(x_chunks), True)
    saved_t = attend(normed_t, qkv_t, FRAMES)
    context_t = saved_t[2]
    attn_term = rows_term(context_t, temporal_output_weight.T)
    attn_term, u_chunks = lax.optimization_barrier((attn_term, u_chunks))
    attn_pieces = exchange(attn_term)
    u_other = swap(u_chunks)
    x_own = own_rows(x_chunks)
    inverse_own, centered_own = normalize(x_own)
    attn_pieces = along(attn_pieces, u_other, inverse_own, centered_own)

    middle_own = half(wide(x_own) + rows_sum(attn_pieces))
    inverse_m, centered_m = normalize(middle_own)
    normed_own = half(centered_m)
    normed_m = spread(normed_own)
    upstream = rows_of_chunks(*after((u_chunks, u_other), normed_own), False)
    d_act = mm_nt(upstream, down_weight)
    normed_m = both(along(normed_m, d_act))
    d_pre, hidden = mlp(*normed_m, up_weight, d_act)
    d_norm_m = rows_term(d_pre, up_weight)
    m_pieces = exchange(d_norm_m)
    left_m, hidden = after((normed_m, hidden), d_norm_m)
    sum_m = Sum(True), Sum(False)
    sent_m = [
        sum_m[0].start(((left_m, d_pre, 3 * HDIM, 0),)),
        sum_m[1].start((((upstream,), hidden, 3 * HDIM, 0),)),
    ]
    m_pieces = along(m_pieces, *sent_m)
    d_middle_own = normalize_back(own_rows(upstream), inverse_m, centered_m, rows_sum(m_pieces))
    d_middle = spread(d_middle_own)
    sent_m = next_of(sum_m, d_middle_own)
    d_middle = both(along(d_middle, *sent_m))

    d_joined = attend_back(saved_t, *d_middle, temporal_output_weight)
    d_norm_t = rows_term(d_joined, qkv_t)
    t_pieces = exchange(d_norm_t)
    left_t, grad_t = after((normed_t, d_middle), d_norm_t)
    sum_t = Sum(True), Sum(False)
    terms = row_pairs((left_t,), d_joined, grad_t, context_t)
    sent_t = [total.start(pairs) for total, pairs in zip(sum_t, terms)]
    sent_m = next_of(sum_m, d_norm_t)
    t_pieces = along(t_pieces, *sent_t, *sent_m)
    d_temporal_own = normalize_back(d_middle_own, inverse_own, centered_own, rows_sum(t_pieces))

    d_frame_own = lax.all_to_all(d_temporal_own, SEQ, 0, 0, tiled=True)
    s_chunks = gather_cross(after(s_part, d_temporal_own))
    d_frame_own = along(d_frame_own, s_chunks)
    d_frame = spread(d_frame_own)
    s_chunks = after(s_chunks, d_frame_own)
    normed_s = rows_of_chunks(s_chunks, swap(s_chunks), True)
    saved_s = attend(normed_s, qkv_s, PATCHES)
    inverse_own_s, centered_own_s = normalize(own_rows(s_chunks))
    sent_t = next_of(sum_t, d_frame_own)
    sent_m = next_of(sum_m, d_frame_own)
    d_frame = both(along(d_frame, inverse_own_s, centered_own_s, *saved_s, *sent_t, *sent_m))

    d_joined = attend_back(saved_s, *d_frame, spatial_output_weight)
    sum_s = Sum(True), Sum(False)
    terms = row_pairs((normed_s,), d_joined, d_frame, saved_s[2])
    sent_s = [total.start(pairs) for total, pairs in zip(sum_s, terms)]
    d_norm_s = rows_term(along(d_joined, *sent_s), qkv_s)
    s_pieces = exchange(d_norm_s)
    sent_t = next_of(sum_t, d_norm_s)
    grad_up, grad_down = next_of(sum_m, d_norm_s)
    s_pieces = along(s_pieces, grad_up, grad_down, *sent_t)
    sent_s = next_of(sum_s, s_pieces)
    result_own = normalize_back(d_frame_own, inverse_own_s, centered_own_s, rows_sum(s_pieces))
    result = jnp.transpose(result_own.reshape(16, 16, width), (1, 0, 2))
    received = lax.all_to_all(result, TP, 0, 0, tiled=True)
    sent_s = next_of(sum_s, result)
    sent_t = next_of(sum_t, result)
    received = along(received, *sent_t, *sent_s)
    result = jnp.transpose(received.reshape(8, 2, 16, width), (1, 2, 0, 3))
    sent_s = next_of(sum_s, received)
    grad_qkv_t, grad_out_t = row_grads(*next_of(sum_t, sent_s))
    grad_qkv_s, grad_out_s = row_grads(*next_of(sum_s, sent_s))
    return (
        result.reshape(2, 1, PATCHES, width),
        grad_qkv_s,
        grad_out_s,
        grad_qkv_t,
        grad_out_t,
        grad_up,
        grad_down.T,
    )


def solution(mesh):
    fine = Mesh(mesh.devices.reshape(4, 4, 2, 4, 2), SEQ + TP)
    stream = P(None, SEQ, None, TP)
    return jax.shard_map(
        per_device,
        mesh=fine,
        in_specs=(
            stream,
            stream,
            stream,
            P(None, None, TP),
            P(TP, None),
            P(None, None, TP),
            P(TP, None),
            P(None, TP),
            P(TP, None),
        ),
        out_specs=(
            stream,
            P(SEQ, None, TP),
            P(TP, SEQ),
            P(SEQ, None, TP),
            P(TP, SEQ),
            P(SEQ, TP),
            P(TP, SEQ),
        ),
        check_vma=False,
    )
```

```python
import math

import jax
import jax.numpy as jnp
from jax import lax
from jax.sharding import Mesh
from jax.sharding import PartitionSpec as P

D = 3072
HDIM = 128
FRAMES = 16
PATCHES = 128
SEQS = 2
TOKENS = 256
HALF = 128
CHIPS = 8
EPS = 1e-06
ROOT = 0.7978845608028654
CUBIC = 0.044715
SCALE = (SEQS * FRAMES * PATCHES) ** -0.5
SEQ = ("y", "zh")
TP = ("zl", "x", "c")
RING = ("zl", "x")
PAIRS = ((0, 1), (1, 0), (2, 3), (3, 2))
CROSS = ((1, 2), (2, 1), (3, 0), (0, 3))


def gelu_both(pre_act):
    inner = jnp.tanh(ROOT * (pre_act + CUBIC * pre_act * pre_act * pre_act))
    value = 0.5 * pre_act * (1.0 + inner)
    slope = 0.5 * (1.0 + inner) + 0.5 * pre_act * (1.0 - inner * inner) * ROOT * (
        1.0 + 3.0 * CUBIC * pre_act * pre_act
    )
    return value, slope


def dot(left, right, dims):
    return lax.dot_general(left, right, (dims, ((), ())), preferred_element_type=jnp.float32)


def mm(left, right):
    return dot(left, right, ((1,), (0,)))


def mm_nt(left, right):
    return dot(left, right, ((1,), (1,)))


def mm_tn(left, right):
    return dot(left, right, ((0,), (0,)))


def half(values):
    return values.astype(jnp.bfloat16)


def wide(values):
    return values.astype(jnp.float32)


def normalize(values):
    values = wide(values)
    inverse = lax.rsqrt(jnp.mean(values * values, axis=-1, keepdims=True) + EPS)
    return inverse, values * inverse


def normalize_back(residual, inverse, centered, gradient):
    inner = jnp.mean(gradient * centered, axis=-1, keepdims=True)
    return half(wide(residual) + inverse * (gradient - centered * inner))


def swap(values):
    return lax.ppermute(values, "c", [(0, 1), (1, 0)])


def spread(values):
    copies = jnp.broadcast_to(values[None], (CHIPS,) + values.shape)
    return lax.all_to_all(copies, RING, 0, 0, tiled=True)


def join_cores(values):
    theirs = swap(values[1])
    first = lax.axis_index("c") == 0
    low = jnp.where(first, values[0], theirs)
    high = jnp.where(first, theirs, values[0])
    return jnp.concatenate((low, high), axis=1)


def gather_z(values):
    theirs = lax.ppermute(values, "zl", [(0, 1), (1, 0)])
    first = lax.axis_index("zl") == 0
    return jnp.stack((jnp.where(first, values, theirs), jnp.where(first, theirs, values)))[:, None]


def gather_x(values, perm, first):
    theirs = lax.ppermute(values, "x", perm)
    low, high = jnp.where(first, values, theirs), jnp.where(first, theirs, values)
    return jnp.concatenate((low, high), axis=1)


def gather_pairs(values):
    return gather_x(values, PAIRS, lax.axis_index("x") % 2 == 0)


def gather_cross(values):
    values = gather_x(values, CROSS, lax.axis_index("x") < 2)
    return values.reshape((CHIPS,) + values.shape[2:])


def own_first(values):
    core = lax.axis_index("c")
    return jnp.where(core == 0, values, values[::-1])


def both(values):
    values = values.reshape(HALF, D)
    return values, swap(values)


def rows_term(left, right):
    theirs = swap(half(mm_nt(left[HALF:], right)))
    mine = half(mm_nt(left[:HALF], right) + wide(theirs))
    return mine.reshape(CHIPS, HALF // CHIPS, D)


def exchange(pieces):
    return lax.all_to_all(pieces, RING, 0, 0, tiled=True)


def rows_sum(pieces):
    return jnp.sum(wide(pieces), axis=0)


def part(order, blocks):
    flag, one, two = order
    one = jnp.concatenate([blocks[k : k + 1] for k in one])
    two = jnp.concatenate([blocks[k : k + 1] for k in two])
    return jnp.where(flag, one, two), jnp.where(flag, two, one)


def products(order, pairs):
    terms = []
    for left, right, width, spot in pairs:
        left = jnp.concatenate(left, axis=0)
        right = right[:, spot * width : (spot + 1) * width]
        terms.append(half(SCALE * mm_tn(left, right)))
    total = jnp.concatenate(terms, axis=1)
    return part(order, total.reshape(4, D // 4, -1))


def add_and_part(order, kept, came):
    total = half(wide(kept) + wide(came))
    if total.shape[0] == 1:
        total = total.reshape(4, total.shape[1] // 4, total.shape[2])
    return part(order, total)


def beside(chunks):
    return jnp.concatenate([chunks[i] for i in range(CHIPS)], axis=1)


def rows_of_chunks(own, other, norm):
    rows = jnp.concatenate((beside(own), beside(other)), axis=0)
    return half(normalize(rows)[1]) if norm else rows


class Sum:
    def __init__(self, ends):
        self.perms = (PAIRS, CROSS) if ends else (CROSS, PAIRS)
        self.orders = {}
        for axis in ("y", "zh"):
            spot = lax.axis_index(axis)
            even = spot % 2 == 0
            outer = (spot == 0) | (spot == 3)
            if ends:
                self.orders[axis] = (outer, (1, 2), (3, 0)), (even, (0,), (1,))
            else:
                self.orders[axis] = (spot < 2, (2, 3), (0, 1)), (even, (1,), (0,))

    def start(self, pairs):
        self.step = 0
        sent, self.kept = products(self.orders["y"][0], pairs)
        return self.go(sent)

    def go(self, sent):
        axis = "y" if self.step < 2 else "zh"
        self.came = lax.ppermute(sent, axis, self.perms[self.step % 2])
        self.step += 1
        return sent

    def next(self, gate):
        came = after(self.came, gate)
        axis = "y" if self.step < 2 else "zh"
        if self.step == 4:
            return half(wide(self.kept[0]) + wide(came[0]))
        order = self.orders[axis][0 if self.step == 2 else 1]
        sent, self.kept = add_and_part(order, self.kept, came)
        return self.go(sent)


def next_of(sums, gate):
    return [total.next(gate) for total in sums]


def after(values, gate):
    return lax.optimization_barrier((values, gate))[0]


def along(values, *work):
    return lax.optimization_barrier((values,) + work)[0]


def row_grads(first, second):
    projection = jnp.concatenate((first, second[:, :HDIM]), axis=1)
    return projection.reshape(-1, 3, HDIM), second[:, HDIM:].T


def own_rows(values):
    chip = lax.axis_index(RING)
    count = HALF // CHIPS
    if values.ndim == 3:
        return beside(lax.dynamic_slice_in_dim(values, chip * count, count, 1))
    return lax.dynamic_slice_in_dim(values[:HALF], chip * count, count, 0)


def attend(normed, weight, span):
    joined = half(mm(normed, weight))
    query, keyset, values = joined[:, :HDIM], joined[:, HDIM : 2 * HDIM], joined[:, 2 * HDIM :]
    scores = mm_nt(query, keyset) / math.sqrt(HDIM)
    group = jnp.arange(TOKENS) // span
    scores = jnp.where(group[:, None] == group[None, :], scores, -jnp.inf)
    raised = jnp.exp(scores - jnp.max(scores, axis=-1, keepdims=True))
    prob = raised / jnp.sum(raised, axis=-1, keepdims=True)
    return joined, prob, half(mm(half(prob), values))


def attend_back(saved, own, other, output_weight):
    joined, prob, _ = saved
    gradient = jnp.concatenate((own, other), axis=0)
    d_context = half(mm_nt(gradient, output_weight))
    query, keyset, values = joined[:, :HDIM], joined[:, HDIM : 2 * HDIM], joined[:, 2 * HDIM :]
    d_values = half(mm_tn(half(prob), d_context))
    d_probs = mm_nt(d_context, values)
    inner = jnp.sum(prob * d_probs, axis=-1, keepdims=True)
    d_scores = half(prob * (d_probs - inner) / math.sqrt(HDIM))
    d_query = half(mm(d_scores, keyset))
    d_keys = half(mm_tn(d_scores, query))
    return jnp.concatenate((d_query, d_keys, d_values), axis=1)


def mlp(own, other, weight, d_act):
    normed = jnp.concatenate((own, other), axis=0)
    value, slope = gelu_both(mm(normed, weight))
    return half(d_act * slope), half(value)


def row_pairs(normed, d_joined, gradient, context):
    first = ((normed, d_joined, 2 * HDIM, 0),)
    return first, ((normed, d_joined, HDIM, 2), (gradient, context, HDIM, 0))


def per_device(
    spatial_input_rows,
    x_temporal,
    cotangent,
    spatial_query_key_value,
    spatial_output_weight,
    temporal_query_key_value,
    temporal_output_weight,
    up_weight,
    down_weight,
):
    width = D // 16
    qkv_t = temporal_query_key_value.reshape(D, 3 * HDIM)
    qkv_s = spatial_query_key_value.reshape(D, 3 * HDIM)

    pair = jnp.stack((x_temporal[:, 0], cotangent[:, 0])).reshape(2, 2, 16, 8, width)
    pair = jnp.transpose(pair, (2, 0, 1, 3, 4))
    s_part = jnp.transpose(spatial_input_rows.reshape(2, 16, 8, width), (0, 2, 1, 3))
    s_part = join_cores(own_first(s_part.reshape(2, HALF, width)))
    pair, s_part = lax.optimization_barrier((pair, s_part))
    pair = lax.all_to_all(pair, SEQ, 0, 0, tiled=True)
    s_part = gather_pairs(gather_z(s_part))
    pair, qkv_t, qkv_s, s_part = lax.optimization_barrier((pair, qkv_t, qkv_s, s_part))
    pair = jnp.transpose(pair, (2, 1, 3, 0, 4)).reshape(2, 2 * HALF, width)
    pair = join_cores(own_first(pair))
    x_chunks, u_part = lax.optimization_barrier((spread(pair[:HALF]), pair[HALF:]))

    u_chunks = spread(u_part)
    normed_t = rows_of_chunks(x_chunks, swap(x_chunks), True)
    saved_t = attend(normed_t, qkv_t, FRAMES)
    context_t = saved_t[2]
    attn_term = rows_term(context_t, temporal_output_weight.T)
    attn_term, u_chunks = lax.optimization_barrier((attn_term, u_chunks))
    attn_pieces = exchange(attn_term)
    u_other = swap(u_chunks)
    x_own = own_rows(x_chunks)
    inverse_own, centered_own = normalize(x_own)
    attn_pieces = along(attn_pieces, u_other, inverse_own, centered_own)

    middle_own = half(wide(x_own) + rows_sum(attn_pieces))
    inverse_m, centered_m = normalize(middle_own)
    normed_own = half(centered_m)
    normed_m = spread(normed_own)
    upstream = rows_of_chunks(*after((u_chunks, u_other), normed_own), False)
    d_act = mm_nt(upstream, down_weight)
    normed_m = both(along(normed_m, d_act))
    d_pre, hidden = mlp(*normed_m, up_weight, d_act)
    d_norm_m = rows_term(d_pre, up_weight)
    m_pieces = exchange(d_norm_m)
    left_m, hidden = after((normed_m, hidden), d_norm_m)
    sum_m = Sum(True), Sum(False)
    sent_m = [
        sum_m[0].start(((left_m, d_pre, 3 * HDIM, 0),)),
        sum_m[1].start((((upstream,), hidden, 3 * HDIM, 0),)),
    ]
    m_pieces = along(m_pieces, *sent_m)
    d_middle_own = normalize_back(own_rows(upstream), inverse_m, centered_m, rows_sum(m_pieces))
    d_middle = spread(d_middle_own)
    sent_m = next_of(sum_m, d_middle_own)
    d_middle = both(along(d_middle, *sent_m))

    d_joined = attend_back(saved_t, *d_middle, temporal_output_weight)
    d_norm_t = rows_term(d_joined, qkv_t)
    t_pieces = exchange(d_norm_t)
    left_t, grad_t = after((normed_t, d_middle), d_norm_t)
    sum_t = Sum(True), Sum(False)
    terms = row_pairs((left_t,), d_joined, grad_t, context_t)
    sent_t = [total.start(pairs) for total, pairs in zip(sum_t, terms)]
    sent_m = next_of(sum_m, d_norm_t)
    t_pieces = along(t_pieces, *sent_t, *sent_m)
    d_temporal_own = normalize_back(d_middle_own, inverse_own, centered_own, rows_sum(t_pieces))

    d_frame_own = lax.all_to_all(d_temporal_own, SEQ, 0, 0, tiled=True)
    s_chunks = gather_cross(after(s_part, d_temporal_own))
    d_frame_own = along(d_frame_own, s_chunks)
    d_frame = spread(d_frame_own)
    s_chunks = after(s_chunks, d_frame_own)
    normed_s = rows_of_chunks(s_chunks, swap(s_chunks), True)
    saved_s = attend(normed_s, qkv_s, PATCHES)
    inverse_own_s, centered_own_s = normalize(own_rows(s_chunks))
    sent_t = next_of(sum_t, d_frame_own)
    sent_m = next_of(sum_m, d_frame_own)
    d_frame = both(along(d_frame, inverse_own_s, centered_own_s, *saved_s, *sent_t, *sent_m))

    d_joined = attend_back(saved_s, *d_frame, spatial_output_weight)
    sum_s = Sum(True), Sum(False)
    terms = row_pairs((normed_s,), d_joined, d_frame, saved_s[2])
    sent_s = [total.start(pairs) for total, pairs in zip(sum_s, terms)]
    d_norm_s = rows_term(along(d_joined, *sent_s), qkv_s)
    s_pieces = exchange(d_norm_s)
    sent_t = next_of(sum_t, d_norm_s)
    grad_up, grad_down = next_of(sum_m, d_norm_s)
    s_pieces = along(s_pieces, grad_up, grad_down, *sent_t)
    sent_s = next_of(sum_s, s_pieces)
    result_own = normalize_back(d_frame_own, inverse_own_s, centered_own_s, rows_sum(s_pieces))
    result = jnp.transpose(result_own.reshape(16, 16, width), (1, 0, 2))
    received = lax.all_to_all(result, TP, 0, 0, tiled=True)
    sent_s = next_of(sum_s, result)
    sent_t = next_of(sum_t, result)
    received = along(received, *sent_t, *sent_s)
    result = jnp.transpose(received.reshape(8, 2, 16, width), (1, 2, 0, 3))
    sent_s = next_of(sum_s, received)
    grad_qkv_t, grad_out_t = row_grads(*next_of(sum_t, sent_s))
    grad_qkv_s, grad_out_s = row_grads(*next_of(sum_s, sent_s))
    return (
        result.reshape(2, 1, PATCHES, width),
        grad_qkv_s,
        grad_out_s,
        grad_qkv_t,
        grad_out_t,
        grad_up,
        grad_down.T,
    )


def solution(mesh):
    fine = Mesh(mesh.devices.reshape(4, 4, 2, 4, 2), SEQ + TP)
    stream = P(None, SEQ, None, TP)
    return jax.shard_map(
        per_device,
        mesh=fine,
        in_specs=(
            stream,
            stream,
            stream,
            P(None, None, TP),
            P(TP, None),
            P(None, None, TP),
            P(TP, None),
            P(None, TP),
            P(TP, None),
        ),
        out_specs=(
            stream,
            P(SEQ, None, TP),
            P(TP, SEQ),
            P(SEQ, None, TP),
            P(TP, SEQ),
            P(SEQ, TP),
            P(TP, SEQ),
        ),
        check_vma=False,
    )
```
